256 devices in a mesh: clip: 2 (over y_lo), seq: 128 (over y_hi, x, z, core).
Axes of the slice: x: 4, y: 4 (y_hi: 2, y_lo: 2; y = y_hi * 2 + y_lo), z: 8, core: 2. Of those that a mesh axis runs over, the one named last changes fastest.
Arguments:
- clips_x: bfloat16 [8, 32768, 1280], P('clip', 'seq'), parts along dimension 0, may hold values from -6 to 6
- slot_phi: bfloat16 [1280, 256], replicated, may hold values from -38.572173 to 38.572173
- w_in: bfloat16 [1280, 163840], P(None, 'seq'), may hold values from -0.875 to 0.875
- b_in: bfloat16 [163840], P('seq'), may hold values from -1.5 to 1.5
- w_out: bfloat16 [163840, 1280], P('seq'), may hold values from -0.125 to 0.125
- b_out: bfloat16 [64, 1280], replicated, may hold values from -1.5 to 1.5
Outputs:
- mixed: bfloat16 [8, 32768, 1280], P('clip', 'seq'), parts along dimension 0
The draws below stay inside these ranges and needn't reach their ends.
There are 2 independent parts, one for each index of `clip`. The reference program is written for one: setup_inputs(seed, part) draws one part's arguments, and reference() takes and returns one part's arrays. A program takes and returns all parts, laid end to end along the dimension named above; an argument that names none is the same for every part. Nothing has to cross between parts.
All inputs are finite; a program needn't handle non-finite values.
Results may differ from the reference program's by a relative error of at most 0.014.
Values may be sent and summed in bfloat16 or wider, within the bound.
No kernel may reach another device: no remote copies, remote signals or barrier semaphores. Data moves between devices by JAX's collectives and lax.ppermute only.
A program may use at most 128 MiB of HBM per device.

```python
import math
import jax
import jax.numpy as jnp

D = 1280
FF = 2560
SLOTS = 4
CLIPS = 4
TOK_DEV = 256
EXPERTS = 64
SLOTS_ALL = 256
TOKENS = 32768


def draw_clips_x(key, part):
    key = jax.random.fold_in(key, 5)
    first, second = jax.random.split(key)
    frames = TOKENS // TOK_DEV
    noise = jax.random.normal(first, (CLIPS, frames, TOK_DEV, D), jnp.float32) * 1.5
    shared = jax.random.normal(second, (CLIPS, frames, 1, D), jnp.float32) * 0.4
    values = jnp.clip(noise + shared, -6.0, 6.0)
    return values.reshape(CLIPS, TOKENS, D).astype(jnp.bfloat16)


def draw_slot_phi(key, part):
    key = jax.random.fold_in(key, 11)
    first = jax.random.fold_in(key, 0)
    base = jnp.clip(jax.random.normal(first, (D, SLOTS_ALL), jnp.float32), -6.0, 6.0) * (1.15 / math.sqrt(D))
    return base.astype(jnp.bfloat16)


def level_of(own_key, extent, cuts, smallest, high):
    def one(dim, blocks):
        heights = jax.random.uniform(jax.random.fold_in(jax.random.fold_in(own_key, 6), dim), (blocks,), jnp.float32, smallest / len(cuts), high / len(cuts))
        return jnp.repeat(jnp.exp(heights), extent[dim] // blocks).reshape((-1,) + (1,) * (len(extent) - dim - 1))

    factor_of = one(*cuts[0])
    for cut in cuts[1:]:
        factor_of = factor_of * one(*cut)
    return factor_of


def normal_values(rng, dims, spread, limit, shards=(), held_as=jnp.bfloat16):
    level = level_of(rng, dims, shards, -0.22, 0.18) if shards else 1.0
    values = jax.random.normal(rng, dims, jnp.float32) * spread * level
    return jnp.minimum(jnp.maximum(values, -limit), limit).astype(held_as)


def setup_inputs(seed: int = 0, part: int = 0) -> dict:
    key_list = jax.random.split(jax.random.key(seed), 7)
    part_splits = jax.random.split(jax.random.fold_in(key_list[6], part), 7)
    return {
        "clips_x": draw_clips_x(jax.random.fold_in(jax.random.fold_in(key_list[6], part), 71), part),
        "slot_phi": draw_slot_phi(jax.random.fold_in(key_list[6], 71), part),
        "w_in": normal_values(key_list[2], (D, EXPERTS * FF), (D // 25) ** -0.5, 0.875, ((1, 128),)),
        "b_in": normal_values(key_list[3], (EXPERTS * FF,), 0.25, 1.5, ((0, 128),)),
        "w_out": normal_values(key_list[4], (EXPERTS * FF, D), FF ** -0.5, 0.125, ((0, 128),)),
        "b_out": normal_values(key_list[5], (EXPERTS, D), 0.25, 1.5),
    }


def reference(clips_x, slot_phi, w_in, b_in, w_out, b_out):
    xf = clips_x.astype(jnp.float32)
    logits = jnp.einsum('ctd,dj->ctj', xf, slot_phi.astype(jnp.float32))
    col_max = jnp.max(logits, axis=1, keepdims=True)
    expo = jnp.exp(logits - col_max)
    col_total = jnp.sum(expo, axis=1)
    dispatch = expo.astype(jnp.bfloat16)
    numer = jnp.einsum('ctj,ctd->cjd', dispatch.astype(jnp.float32), xf)
    slot_in = (numer / col_total[:, :, None]).astype(jnp.bfloat16)
    grouped = slot_in.reshape(CLIPS, EXPERTS, SLOTS, D).astype(jnp.float32)
    first = w_in.reshape(D, EXPERTS, FF).astype(jnp.float32)
    pre = jnp.einsum('cesd,def->cesf', grouped, first)
    pre = pre + b_in.reshape(EXPERTS, FF)[None, :, None, :].astype(jnp.float32)
    hidden = jax.nn.gelu(pre, approximate=False).astype(jnp.bfloat16)
    second = w_out.reshape(EXPERTS, FF, D).astype(jnp.float32)
    result = jnp.einsum('cesf,efd->cesd', hidden.astype(jnp.float32), second)
    result = result + b_out[None, :, None, :].astype(jnp.float32)
    slot_out = result.astype(jnp.bfloat16).reshape(CLIPS, SLOTS_ALL, D)
    row_max = jnp.max(logits, axis=2, keepdims=True)
    weights = jnp.exp(logits - row_max)
    comb = (weights / jnp.sum(weights, axis=2, keepdims=True)).astype(jnp.bfloat16)
    mixed = jnp.einsum('ctj,cjd->ctd', comb.astype(jnp.float32), slot_out.astype(jnp.float32))
    return mixed.astype(jnp.bfloat16)
```

```python
import jax
import jax.numpy as jnp
from jax import lax
from jax.sharding import PartitionSpec as P

LANES = 128


def coords(index):
    return index // 64, index // 16 % 4, index // 2 % 8, index % 2


def groups_by(key):
    found = {}
    for index in range(128):
        found.setdefault(key(*coords(index)), []).append(index)
    return list(found.values())


ALONG_X = groups_by(lambda y, x, z, core: (y, z, core))
ALONG_YZ = groups_by(lambda y, x, z, core: (x, core))


def exchange(value, groups):
    return lax.all_to_all(value, "seq", 0, 0, tiled=True, axis_index_groups=groups)


def swap_cores(value):
    return lax.ppermute(value, "seq", [(source, source ^ 1) for source in range(128)])


def short(value):
    return lax.reduce_precision(value, 8, 7)


def with_stats(numer, peak, total):
    p1 = short(peak)
    p2 = short(peak - p1)
    p3 = peak - p1 - p2
    t1 = short(total)
    t2 = total - t1
    pad = jnp.zeros(peak.shape[:-1] + (LANES - 5,), jnp.float32)
    return jnp.concatenate([numer, p1, p2, p3, t1, t2, pad], axis=-1).astype(jnp.bfloat16)


def stats_of(packed):
    s = packed[..., -LANES:].astype(jnp.float32)
    return s[..., 0:1] + s[..., 1:2] + s[..., 2:3], s[..., 3:4] + s[..., 4:5]


def merged(packed):
    peaks, totals = stats_of(packed)
    peak = jnp.max(peaks, axis=0)
    factor = jnp.exp(peaks - peak)
    total = jnp.sum(factor * totals, axis=0)
    numer = jnp.sum(factor * packed[..., :-LANES].astype(jnp.float32), axis=0)
    return numer, peak, total


def per_device(clips_x, slot_phi, w_in, b_in, w_out, b_out):
    clips, tokens, width = clips_x.shape
    half = width // 2
    me = lax.axis_index("seq")
    core = me % 2
    mine = core * half
    theirs = half - mine
    logits = jnp.einsum("dj,ctd->cjt", slot_phi, clips_x, preferred_element_type=jnp.float32)
    peak = jnp.max(logits, axis=2, keepdims=True)
    expo = jnp.exp(logits - peak)
    total = jnp.sum(expo, axis=2, keepdims=True)
    dispatch = expo.astype(jnp.bfloat16)

    def sums(start):
        part = lax.dynamic_slice_in_dim(clips_x, start, half, 2)
        return jnp.einsum("cjt,ctd->cjd", dispatch, part, preferred_element_type=jnp.float32)

    arrived = swap_cores(with_stats(sums(theirs), peak, total))
    own = sums(mine)
    other_peak, other_total = stats_of(arrived)
    top = jnp.maximum(peak, other_peak)
    f_own = jnp.exp(peak - top)
    f_other = jnp.exp(other_peak - top)
    numer = f_own * own + f_other * arrived[..., :-LANES].astype(jnp.float32)
    packed = with_stats(numer, top, f_own * total + f_other * other_total)
    packed = packed.reshape(clips, 2, 4, 32, half + LANES).transpose(2, 0, 1, 3, 4)
    packed = exchange(packed.reshape(4, clips * 64, half + LANES), ALONG_X)
    packed = with_stats(*merged(packed.reshape(4, clips * 64, half + LANES)))
    packed = packed.reshape(clips, 16, 4, half + LANES).transpose(1, 0, 2, 3)
    packed = exchange(packed.reshape(16, clips * 4, half + LANES), ALONG_YZ)
    numer, _, total = merged(packed)
    slot_in = (numer / total).astype(jnp.bfloat16)
    partner = swap_cores(slot_in)
    rows = jnp.where(
        core == 0,
        jnp.concatenate([slot_in, partner], axis=1),
        jnp.concatenate([partner, slot_in], axis=1),
    )
    pre = jnp.dot(rows, w_in, preferred_element_type=jnp.float32)
    hidden = jax.nn.gelu(pre + b_in.astype(jnp.float32), approximate=False).astype(jnp.bfloat16)
    partial = jnp.dot(hidden, w_out, preferred_element_type=jnp.float32)
    part_mine = jnp.where(core == 0, partial[:, :half], partial[:, half:])
    part_theirs = jnp.where(core == 0, partial[:, half:], partial[:, :half])
    bias = lax.dynamic_slice(b_out, (me // 2, mine), (1, half)).astype(jnp.float32)
    summed = part_mine + swap_cores(part_theirs.astype(jnp.bfloat16)).astype(jnp.float32)
    slot_out = (summed + bias).astype(jnp.bfloat16)
    gathered = exchange(jnp.broadcast_to(slot_out[None], (16,) + slot_out.shape), ALONG_YZ)
    gathered = gathered.reshape(16, clips, 4, half).transpose(1, 0, 2, 3).reshape(1, clips * 64, half)
    gathered = exchange(jnp.broadcast_to(gathered, (4, clips * 64, half)), ALONG_X)
    gathered = gathered.reshape(4, clips, 2, 32, half).transpose(1, 2, 0, 3, 4).reshape(clips, 256, half)
    other = swap_cores(gathered)
    row_max = jnp.max(logits, axis=1, keepdims=True)
    weights = jnp.exp(logits - row_max)
    comb = (weights / jnp.sum(weights, axis=1, keepdims=True)).astype(jnp.bfloat16)

    def mix(values):
        return jnp.einsum("cjt,cjd->ctd", comb, values, preferred_element_type=jnp.float32).astype(jnp.bfloat16)

    a, b = mix(gathered), mix(other)
    return jnp.where(core == 0, jnp.concatenate([a, b], axis=2), jnp.concatenate([b, a], axis=2))


def solution(mesh):
    placed = (P("clip", "seq", None), P(), P(None, "seq"), P("seq"), P("seq", None), P())
    return jax.shard_map(
        per_device, mesh=mesh, in_specs=placed, out_specs=P("clip", "seq", None), check_vma=False
    )
```

```python
import jax
import jax.numpy as jnp
from jax import lax
from jax.experimental import pallas as pl
from jax.experimental.pallas import tpu as pltpu
from jax.sharding import PartitionSpec as P

BF16 = jnp.bfloat16
F32 = jnp.float32
CLIPS = 4
SLOTS = 256
TOK = 256
D = 1280
HALF = 640
STATS = CLIPS * HALF
ROW = STATS + 128
VMEM_LIMIT = 40 * 2**20


def coords(index):
    return index // 64, index // 16 % 4, index // 2 % 8, index % 2


def groups_by(key):
    found = {}
    for index in range(128):
        found.setdefault(key(*coords(index)), []).append(index)
    return list(found.values())


ALONG_X = groups_by(lambda y, x, z, core: (y, z, core))
ALONG_YZ = groups_by(lambda y, x, z, core: (x, core))


def exchange(value, groups):
    return lax.all_to_all(value, "seq", 0, 0, tiled=True, axis_index_groups=groups)


def swap_cores(value):
    return lax.ppermute(value, "seq", [(source, source ^ 1) for source in range(128)])


def params():
    return pltpu.CompilerParams(vmem_limit_bytes=VMEM_LIMIT)


def cost(flops, bytes_accessed):
    return pl.CostEstimate(flops=flops, bytes_accessed=bytes_accessed, transcendentals=0)


def stats_lanes(clip, peak, total):
    p1 = peak.astype(BF16).astype(F32)
    p2 = (peak - p1).astype(BF16).astype(F32)
    p3 = peak - p1 - p2
    t1 = total.astype(BF16).astype(F32)
    t2 = total - t1
    lane = lax.broadcasted_iota(jnp.int32, (peak.shape[0], 128), 1) - 8 * clip
    out = jnp.where(lane == 0, p1, 0.0)
    for k, column in enumerate((p2, p3, t1, t2)):
        out = jnp.where(lane == k + 1, column, out)
    return out


def read_stats(clip, stats):
    lane = lax.broadcasted_iota(jnp.int32, stats.shape, stats.ndim - 1) - 8 * clip
    peak = jnp.sum(jnp.where((lane >= 0) & (lane < 3), stats, 0.0), axis=-1, keepdims=True)
    total = jnp.sum(jnp.where((lane >= 3) & (lane < 5), stats, 0.0), axis=-1, keepdims=True)
    return peak, total


def keep_stats(clip, lanes, scratch):
    @pl.when(clip == 0)
    def _():
        scratch[...] = lanes

    @pl.when(clip > 0)
    def _():
        scratch[...] += lanes

    return scratch[...].astype(BF16)


def columns(clip):
    return pl.ds(pl.multiple_of(clip * HALF, 128), HALF)


def dispatch_kernel(core_ref, x_ref, phi_ref, send_ref, logits_ref, dispatch_ref, scratch):
    clip = pl.program_id(0)
    logits = jnp.dot(x_ref[0], phi_ref[...], preferred_element_type=F32)
    logits_ref[0] = logits
    turned = logits.T
    peak = jnp.max(turned, axis=1, keepdims=True)
    expo = jnp.exp(turned - peak)
    total = jnp.sum(expo, axis=1, keepdims=True)
    dispatch = expo.astype(BF16)
    dispatch_ref[0] = dispatch
    other = x_ref[0, :, columns(1 - core_ref[0])]
    send_ref[:, columns(clip)] = jnp.dot(dispatch, other, preferred_element_type=F32).astype(BF16)
    send_ref[:, STATS:] = keep_stats(clip, stats_lanes(clip, peak, total), scratch)


def dispatch_call(core, clips_x, slot_phi):
    return pl.pallas_call(
        dispatch_kernel,
        out_shape=(
            jax.ShapeDtypeStruct((SLOTS, ROW), BF16),
            jax.ShapeDtypeStruct((CLIPS, TOK, SLOTS), F32),
            jax.ShapeDtypeStruct((CLIPS, SLOTS, TOK), BF16),
        ),
        grid_spec=pltpu.PrefetchScalarGridSpec(
            num_scalar_prefetch=1,
            grid=(CLIPS,),
            in_specs=[
                pl.BlockSpec((1, TOK, D), lambda c, core: (c, 0, 0)),
                pl.BlockSpec((D, SLOTS), lambda c, core: (0, 0)),
            ],
            out_specs=(
                pl.BlockSpec((SLOTS, ROW), lambda c, core: (0, 0)),
                pl.BlockSpec((1, TOK, SLOTS), lambda c, core: (c, 0, 0)),
                pl.BlockSpec((1, SLOTS, TOK), lambda c, core: (c, 0, 0)),
            ),
            scratch_shapes=[pltpu.VMEM((SLOTS, 128), F32)],
        ),
        compiler_params=params(),
        cost_estimate=cost(2 * 1024 * 256 * 1920, 6 * 2**20),
        name="dispatch",
    )(core, clips_x, slot_phi)


def own_kernel(core_ref, x_ref, logits_ref, dispatch_ref, own_ref, comb_ref):
    own_ref[...] = jnp.dot(dispatch_ref[0], x_ref[0], preferred_element_type=F32)
    logits = logits_ref[0]
    weights = jnp.exp(logits - jnp.max(logits, axis=1, keepdims=True))
    comb_ref[0] = (weights / jnp.sum(weights, axis=1, keepdims=True)).astype(BF16)


def own_call(core, clips_x, logits, dispatch):
    return pl.pallas_call(
        own_kernel,
        out_shape=(
            jax.ShapeDtypeStruct((SLOTS, CLIPS * HALF), F32),
            jax.ShapeDtypeStruct((CLIPS, TOK, SLOTS), BF16),
        ),
        grid_spec=pltpu.PrefetchScalarGridSpec(
            num_scalar_prefetch=1,
            grid=(CLIPS,),
            in_specs=[
                pl.BlockSpec((1, TOK, HALF), lambda c, core: (c, 0, core[0])),
                pl.BlockSpec((1, TOK, SLOTS), lambda c, core: (c, 0, 0)),
                pl.BlockSpec((1, SLOTS, TOK), lambda c, core: (c, 0, 0)),
            ],
            out_specs=(
                pl.BlockSpec((SLOTS, HALF), lambda c, core: (0, c)),
                pl.BlockSpec((1, TOK, SLOTS), lambda c, core: (c, 0, 0)),
            ),
        ),
        compiler_params=params(),
        cost_estimate=cost(2 * 1024 * 256 * 640, 6 * 2**20),
        name="own_half",
    )(core, clips_x, logits, dispatch)


def merge_cores_kernel(own_ref, mine_ref, arrived_ref, theirs_ref, out_ref, scratch):
    clip = pl.program_id(0)
    peak_a, total_a = read_stats(clip, mine_ref[...].astype(F32))
    peak_b, total_b = read_stats(clip, theirs_ref[...].astype(F32))
    peak = jnp.maximum(peak_a, peak_b)
    fa = jnp.exp(peak_a - peak)
    fb = jnp.exp(peak_b - peak)
    value = (fa * own_ref[...] + fb * arrived_ref[...].astype(F32)).astype(BF16)
    stats = keep_stats(clip, stats_lanes(clip, peak, fa * total_a + fb * total_b), scratch)
    for y in range(2):
        for x in range(4):
            rows = slice((y * 4 + x) * 32, (y * 4 + x) * 32 + 32)
            out_ref[x, y * 32 : y * 32 + 32, columns(clip)] = value[rows]
            out_ref[x, y * 32 : y * 32 + 32, STATS:] = stats[rows]


def merge_cores_call(own, sent, arrived):
    return pl.pallas_call(
        merge_cores_kernel,
        out_shape=jax.ShapeDtypeStruct((4, 64, ROW), BF16),
        grid=(CLIPS,),
        in_specs=[
            pl.BlockSpec((SLOTS, HALF), lambda c: (0, c)),
            pl.BlockSpec((SLOTS, 128), lambda c: (0, STATS // 128)),
            pl.BlockSpec((SLOTS, HALF), lambda c: (0, c)),
            pl.BlockSpec((SLOTS, 128), lambda c: (0, STATS // 128)),
        ],
        out_specs=pl.BlockSpec((4, 64, ROW), lambda c: (0, 0, 0)),
        scratch_shapes=[pltpu.VMEM((SLOTS, 128), F32)],
        compiler_params=params(),
        cost_estimate=cost(2**20, 6 * 2**20),
        name="merge_cores",
    )(own, sent, arrived, arrived)


def merge(clip, sources, value_of, stats_of):
    stats = [read_stats(clip, stats_of(k)) for k in range(sources)]
    peak = stats[0][0]
    for p, _ in stats[1:]:
        peak = jnp.maximum(peak, p)
    value, total = None, None
    for k, (p, t) in enumerate(stats):
        factor = jnp.exp(p - peak)
        v = factor * value_of(k)
        value = v if k == 0 else value + v
        total = factor * t if k == 0 else total + factor * t
    return value, peak, total


def merge_x_kernel(value_ref, stats_ref, out_ref, scratch):
    clip = pl.program_id(0)
    value, peak, total = merge(
        clip, 4, lambda k: value_ref[k].astype(F32), lambda k: stats_ref[k].astype(F32)
    )
    value = value.astype(BF16)
    stats = keep_stats(clip, stats_lanes(clip, peak, total), scratch)
    for piece in range(16):
        rows = slice(piece * 4, piece * 4 + 4)
        out_ref[piece, :, columns(clip)] = value[rows]
        out_ref[piece, :, STATS:] = stats[rows]


def merge_x_call(arrived):
    return pl.pallas_call(
        merge_x_kernel,
        out_shape=jax.ShapeDtypeStruct((16, 4, ROW), BF16),
        grid=(CLIPS,),
        in_specs=[
            pl.BlockSpec((4, 64, HALF), lambda c: (0, 0, c)),
            pl.BlockSpec((4, 64, 128), lambda c: (0, 0, STATS // 128)),
        ],
        out_specs=pl.BlockSpec((16, 4, ROW), lambda c: (0, 0, 0)),
        scratch_shapes=[pltpu.VMEM((64, 128), F32)],
        compiler_params=params(),
        cost_estimate=cost(2**20, 2 * 2**20),
        name="merge_x",
    )(arrived, arrived)


def merge_yz_kernel(value_ref, out_ref):
    for clip in range(CLIPS):
        value, _, total = merge(
            clip,
            16,
            lambda k: value_ref[k, :, clip * HALF : clip * HALF + HALF].astype(F32),
            lambda k: value_ref[k, :, STATS:].astype(F32),
        )
        out_ref[clip] = (value / total).astype(BF16)


def merge_yz_call(arrived):
    return pl.pallas_call(
        merge_yz_kernel,
        out_shape=jax.ShapeDtypeStruct((CLIPS, 4, HALF), BF16),
        compiler_params=params(),
        cost_estimate=cost(2**20, 2**19),
        name="merge_yz",
    )(arrived)


def spread_kernel(value_ref, out_ref):
    for x in range(4):
        for piece in range(16):
            out_ref[x, piece * 4 : piece * 4 + 4, :] = value_ref[piece]


def spread_call(value):
    return pl.pallas_call(
        spread_kernel,
        out_shape=jax.ShapeDtypeStruct((4, 64, CLIPS * HALF), BF16),
        compiler_params=params(),
        cost_estimate=cost(2**18, 2 * 2**20),
        name="spread_x",
    )(value)


def mix_kernel(side_ref, comb_ref, slots_ref, *rest):
    out_ref = rest[-1]
    pieces = [slots_ref[x, y * 32 : y * 32 + 32, :] for y in range(2) for x in range(4)]
    slots = jnp.concatenate(pieces, axis=0)
    out_ref[0] = jnp.dot(comb_ref[0], slots, preferred_element_type=F32).astype(BF16)


def mix_call(side, comb, slots, base=None):
    more = [] if base is None else [base]
    return pl.pallas_call(
        mix_kernel,
        out_shape=jax.ShapeDtypeStruct((CLIPS, TOK, D), BF16),
        grid_spec=pltpu.PrefetchScalarGridSpec(
            num_scalar_prefetch=1,
            grid=(CLIPS,),
            in_specs=[
                pl.BlockSpec((1, TOK, SLOTS), lambda c, side: (c, 0, 0)),
                pl.BlockSpec((4, 64, HALF), lambda c, side: (0, 0, c)),
            ]
            + [pl.BlockSpec(memory_space=pl.ANY)] * len(more),
            out_specs=pl.BlockSpec((1, TOK, HALF), lambda c, side: (c, 0, side[0])),
        ),
        input_output_aliases={3: 0} if more else {},
        compiler_params=params(),
        cost_estimate=cost(2 * 1024 * 256 * 640, 4 * 2**20),
        name="mix",
    )(side, comb, slots, *more)


def per_device(clips_x, slot_phi, w_in, b_in, w_out, b_out):
    me = lax.axis_index("seq")
    core = (me % 2).astype(jnp.int32)
    mine = core * HALF
    core_ref = core[None]
    sent, logits, dispatch = dispatch_call(core_ref, clips_x, slot_phi)
    arrived = swap_cores(sent)
    own, comb = own_call(core_ref, clips_x, logits, dispatch)
    packed = merge_cores_call(own, sent, arrived)
    packed = exchange(packed, ALONG_X)
    packed = merge_x_call(packed)
    packed = exchange(packed, ALONG_YZ)
    slot_in = merge_yz_call(packed).reshape(CLIPS * 4, HALF)
    partner = swap_cores(slot_in)
    rows = jnp.where(
        core == 0,
        jnp.concatenate([slot_in, partner], axis=1),
        jnp.concatenate([partner, slot_in], axis=1),
    )
    pre = jnp.dot(rows, w_in, preferred_element_type=F32)
    hidden = jax.nn.gelu(pre + b_in.astype(F32), approximate=False).astype(BF16)
    partial = jnp.dot(hidden, w_out, preferred_element_type=F32)
    part_mine = jnp.where(core == 0, partial[:, :HALF], partial[:, HALF:])
    part_theirs = jnp.where(core == 0, partial[:, HALF:], partial[:, :HALF])
    bias = lax.dynamic_slice(b_out, (me // 2, mine), (1, HALF)).astype(F32)
    summed = part_mine + swap_cores(part_theirs.astype(BF16)).astype(F32)
    slot_out = (summed + bias).astype(BF16)
    slot_out = slot_out.reshape(CLIPS, 4, HALF).transpose(1, 0, 2).reshape(1, 4, CLIPS * HALF)
    gathered = exchange(jnp.broadcast_to(slot_out, (16, 4, CLIPS * HALF)), ALONG_YZ)
    gathered = exchange(spread_call(gathered), ALONG_X)
    other = swap_cores(gathered)
    mixed = mix_call(core_ref, comb, gathered)
    return mix_call(1 - core_ref, comb, other, mixed)


def solution(mesh):
    placed = (P("clip", "seq", None), P(), P(None, "seq"), P("seq"), P("seq", None), P())
    return jax.shard_map(
        per_device, mesh=mesh, in_specs=placed, out_specs=P("clip", "seq", None), check_vma=False
    )
```

```python
import functools

import jax
import jax.numpy as jnp
from jax import lax
from jax.experimental import pallas as pl
from jax.experimental.pallas import tpu as pltpu
from jax.sharding import PartitionSpec as P

BF16 = jnp.bfloat16
F32 = jnp.float32
CLIPS = 4
SLOTS = 256
TOK = 256
D = 1280
HALF = 640
STATS = CLIPS * HALF
ROW = STATS + 128
VMEM_LIMIT = 8 * 2**20
DISPATCH_VMEM = 49 * 2**20


def coords(index):
    return index // 64, index // 16 % 4, index // 2 % 8, index % 2


def groups_by(key):
    found = {}
    for index in range(128):
        found.setdefault(key(*coords(index)), []).append(index)
    return list(found.values())


STAGE_TWO = groups_by(lambda y, x, z, core: (core, x) if core == 0 else (core, y, z % 2))


def peer(index, k):
    y, x, z, core = coords(index)
    if core == 0:
        x = (x + (0, 1, 3, 2)[k]) % 4
    else:
        y, z = y ^ (k // 2), z ^ (k % 2)
    return ((y * 4 + x) * 8 + z) * 2 + core


def exchange(value, groups):
    return lax.all_to_all(value, "seq", 0, 0, tiled=True, axis_index_groups=groups)


def swap_cores(value):
    return lax.ppermute(value, "seq", [(source, source ^ 1) for source in range(128)])


def send_piece(value, k):
    return lax.ppermute(value, "seq", [(source, peer(source, k)) for source in range(128)])


def params(limit=VMEM_LIMIT):
    return pltpu.CompilerParams(vmem_limit_bytes=limit)


def cost(flops, bytes_accessed):
    return pl.CostEstimate(flops=flops, bytes_accessed=bytes_accessed, transcendentals=0)


DISPATCH_COST = cost(2 * 1024 * 256 * 1920, 6 * 2**20)


def stats_lanes(clip, peak, total):
    p1 = peak.astype(BF16).astype(F32)
    p2 = (peak - p1).astype(BF16).astype(F32)
    p3 = peak - p1 - p2
    t1 = total.astype(BF16).astype(F32)
    t2 = total - t1
    lane = lax.broadcasted_iota(jnp.int32, (peak.shape[0], 128), 1) - 8 * clip
    out = jnp.where(lane == 0, p1, 0.0)
    for k, column in enumerate((p2, p3, t1, t2)):
        out = jnp.where(lane == k + 1, column, out)
    return out


def read_stats(clip, stats):
    lane = lax.broadcasted_iota(jnp.int32, stats.shape, stats.ndim - 1) - 8 * clip
    peak = jnp.sum(jnp.where((lane >= 0) & (lane < 3), stats, 0.0), axis=-1, keepdims=True)
    total = jnp.sum(jnp.where((lane >= 3) & (lane < 5), stats, 0.0), axis=-1, keepdims=True)
    return peak, total


def column_slice(clip):
    return slice(clip * HALF, clip * HALF + HALF)


def dynamic_half(core):
    return pl.ds(pl.multiple_of(core * HALF, 128), HALF)


def phi_rows(core):
    return pl.ds(pl.multiple_of(core * HALF, 128), HALF)


def order_matrix(core, where_ref, start):
    row = lax.broadcasted_iota(jnp.int32, (SLOTS, 1), 0)
    k, rest = row >> 6, row & 63
    piece = jnp.where(
        k < 2,
        jnp.where(k == 0, where_ref[start], where_ref[start + 1]),
        jnp.where(k == 2, where_ref[start + 2], where_ref[start + 3]),
    )
    by_x = ((rest >> 5) << 7) | (piece << 5) | (rest & 31)
    by_yz = ((piece >> 1) << 7) | ((rest >> 4) << 5) | (((rest >> 2) & 3) << 3) | ((piece & 1) << 2) | (rest & 3)
    slot = jnp.where(core == 0, by_x, by_yz)
    return jnp.where(lax.broadcasted_iota(jnp.int32, (SLOTS, SLOTS), 1) == slot, 1.0, 0.0).astype(BF16)


VMEM_SPEC = pl.BlockSpec(memory_space=pltpu.VMEM)
SMEM_SPEC = pl.BlockSpec(memory_space=pltpu.SMEM)
HBM_SPEC = pl.BlockSpec(memory_space=pltpu.HBM)
SENT, OTHER_SENT, GOT, OTHER_GOT = 1, 5, 9, 13
SEND_ORDER = (3, 1, 2, 0)


def dispatch_kernel(where_ref, x_hbm, phi_hbm, *refs):
    send_refs, (logits_ref, dispatch_ref, x_ref, other_ref, phi_ref, x_sem, phi_sem) = refs[:4], refs[4:]
    core = where_ref[0]
    phi_copy = pltpu.make_async_copy(phi_hbm, phi_ref, phi_sem)
    phi_copy.start()
    copies = []
    for clip in range(CLIPS):
        for side, target in ((core, x_ref), (1 - core, other_ref)):
            source = x_hbm.at[clip, :, dynamic_half(side)]
            copies.append(pltpu.make_async_copy(source, target.at[clip], x_sem.at[len(copies)]))
            copies[-1].start()
    order = order_matrix(1 - core, where_ref, OTHER_SENT)
    phi_copy.wait()
    phi = jnp.concatenate([phi_ref[phi_rows(core), :], phi_ref[phi_rows(1 - core), :]], axis=0)
    for copy in copies:
        copy.wait()
    tokens = jnp.concatenate(
        [x_ref[...].reshape(CLIPS * TOK, HALF), other_ref[...].reshape(CLIPS * TOK, HALF)], axis=1
    )
    all_logits = jnp.dot(tokens, phi, preferred_element_type=F32)
    stats = jnp.zeros((SLOTS, 128), F32)
    for clip in range(CLIPS):
        logits = all_logits[clip * TOK : clip * TOK + TOK]
        logits_ref[clip] = logits
        peak = jnp.max(logits, axis=0, keepdims=True)
        expo = jnp.exp(logits - peak)
        total = jnp.sum(expo, axis=0, keepdims=True)
        dispatch = lax.dot_general(
            order, expo.astype(BF16), (((1,), (1,)), ((), ())), preferred_element_type=F32
        ).astype(BF16)
        dispatch_ref[clip] = dispatch
        sums = jnp.dot(dispatch, other_ref[clip], preferred_element_type=F32).astype(BF16)
        for k in range(4):
            send_refs[k][:, column_slice(clip)] = sums[k * 64 : k * 64 + 64]
        both = jnp.concatenate([peak, total, jnp.zeros((6, SLOTS), F32)], axis=0).T
        stats += stats_lanes(clip, both[:, 0:1], both[:, 1:2])
    stats = jnp.dot(order, stats.astype(BF16), preferred_element_type=F32).astype(BF16)
    for k in range(4):
        send_refs[k][:, STATS:] = stats[k * 64 : k * 64 + 64]


def dispatch_call(where, clips_x, slot_phi):
    return pl.pallas_call(
        dispatch_kernel,
        out_shape=tuple(jax.ShapeDtypeStruct((64, ROW), BF16) for _ in range(4))
        + (
            jax.ShapeDtypeStruct((CLIPS, TOK, SLOTS), F32),
            jax.ShapeDtypeStruct((CLIPS, SLOTS, TOK), BF16),
            jax.ShapeDtypeStruct((CLIPS, TOK, HALF), BF16),
        ),
        in_specs=[SMEM_SPEC, HBM_SPEC, HBM_SPEC],
        out_specs=(VMEM_SPEC,) * 7,
        scratch_shapes=[
            pltpu.VMEM((CLIPS, TOK, HALF), BF16),
            pltpu.VMEM((D, SLOTS), BF16),
            pltpu.SemaphoreType.DMA((2 * CLIPS,)),
            pltpu.SemaphoreType.DMA,
        ],
        compiler_params=params(DISPATCH_VMEM),
        cost_estimate=DISPATCH_COST,
        name="dispatch",
    )(where, clips_x, slot_phi)


def own_kernel(where_ref, x_ref, dispatch_ref, s0, s1, s2, s3, own_ref, stats_ref):
    core = where_ref[0]
    given = order_matrix(1 - core, where_ref, OTHER_SENT)
    order = order_matrix(core, where_ref, SENT)
    order = lax.dot_general(order, given, (((1,), (1,)), ((), ())), preferred_element_type=F32).astype(BF16)
    stats = jnp.concatenate([s[:, STATS:] for s in (s0, s1, s2, s3)], axis=0)
    stats_ref[...] = jnp.dot(order, stats, preferred_element_type=F32).astype(BF16)
    for clip in range(CLIPS):
        dispatch = jnp.dot(order, dispatch_ref[clip], preferred_element_type=F32).astype(BF16)
        own_ref[:, column_slice(clip)] = jnp.dot(dispatch, x_ref[clip], preferred_element_type=F32)


def own_call(where, x_half, dispatch, sent):
    return pl.pallas_call(
        own_kernel,
        out_shape=(
            jax.ShapeDtypeStruct((SLOTS, CLIPS * HALF), F32),
            jax.ShapeDtypeStruct((SLOTS, 128), BF16),
        ),
        in_specs=[SMEM_SPEC] + [VMEM_SPEC] * 6,
        out_specs=(VMEM_SPEC,) * 2,
        compiler_params=params(),
        cost_estimate=cost(2 * 1024 * 256 * 640, 6 * 2**20),
        name="own_half",
    )(where, x_half, dispatch, *sent)


def comb_kernel(where_ref, logits_ref, piece_ref, comb_ref, other_comb_ref, same_ref):
    core = where_ref[0]
    same_ref[...] = piece_ref[...]
    orders = order_matrix(core, where_ref, GOT), order_matrix(1 - core, where_ref, OTHER_GOT)
    for clip in range(CLIPS):
        logits = logits_ref[clip]
        weights = jnp.exp(logits - jnp.max(logits, axis=1, keepdims=True))
        comb = (weights / jnp.sum(weights, axis=1, keepdims=True)).astype(BF16)
        for order, out_ref in zip(orders, (comb_ref, other_comb_ref)):
            turned = lax.dot_general(comb, order, (((1,), (1,)), ((), ())), preferred_element_type=F32)
            out_ref[clip] = turned.astype(BF16)


def comb_call(where, logits, piece):
    return pl.pallas_call(
        comb_kernel,
        out_shape=(
            jax.ShapeDtypeStruct((CLIPS, TOK, SLOTS), BF16),
            jax.ShapeDtypeStruct((CLIPS, TOK, SLOTS), BF16),
            jax.ShapeDtypeStruct((64, CLIPS * HALF), BF16),
        ),
        in_specs=[SMEM_SPEC] + [VMEM_SPEC] * 2,
        out_specs=(VMEM_SPEC,) * 3,
        compiler_params=params(),
        cost_estimate=cost(2**27, 4 * 2**20),
        name="comb",
    )(where, logits, piece)


def merge_cores_kernel(k, own_ref, mine_ref, arrived_ref, out_ref):
    rows = slice(k * 64, k * 64 + 64)
    mine = mine_ref[rows].astype(F32)
    theirs = arrived_ref[:, STATS:].astype(F32)
    stats = jnp.zeros(mine.shape, F32)
    for clip in range(CLIPS):
        peak_a, total_a = read_stats(clip, mine)
        peak_b, total_b = read_stats(clip, theirs)
        peak = jnp.maximum(peak_a, peak_b)
        fa = jnp.exp(peak_a - peak)
        fb = jnp.exp(peak_b - peak)
        at = column_slice(clip)
        out_ref[:, at] = (fa * own_ref[rows, at] + fb * arrived_ref[:, at].astype(F32)).astype(BF16)
        stats += stats_lanes(clip, peak, fa * total_a + fb * total_b)
    out_ref[:, STATS:] = stats.astype(BF16)


def merge_cores_call(k, own, mine, arrived):
    return pl.pallas_call(
        functools.partial(merge_cores_kernel, k),
        out_shape=jax.ShapeDtypeStruct((64, ROW), BF16),
        in_specs=[VMEM_SPEC] * 3,
        out_specs=VMEM_SPEC,
        compiler_params=params(),
        cost_estimate=cost(2**20, 2**20),
        name="merge_cores",
    )(own, mine, arrived)


def merge(clip, sources, value_of, stats_of):
    stats = [read_stats(clip, stats_of(k)) for k in range(sources)]
    peak = stats[0][0]
    for p, _ in stats[1:]:
        peak = jnp.maximum(peak, p)
    value, total = None, None
    for k, (p, t) in enumerate(stats):
        factor = jnp.exp(p - peak)
        v = factor * value_of(k)
        value = v if k == 0 else value + v
        total = factor * t if k == 0 else total + factor * t
    return value, peak, total


def merge_four_kernel(*refs):
    piece_refs, out_ref = refs[:4], refs[4]
    all_stats = jnp.zeros((64, 128), F32)
    for clip in range(CLIPS):
        at = column_slice(clip)
        value, peak, total = merge(
            clip,
            4,
            lambda k: piece_refs[k][:, at].astype(F32),
            lambda k: piece_refs[k][:, STATS:].astype(F32),
        )
        value = value.astype(BF16)
        all_stats += stats_lanes(clip, peak, total)
        for piece in range(16):
            out_ref[piece, :, at] = value[piece * 4 : piece * 4 + 4]
    all_stats = all_stats.astype(BF16)
    for piece in range(16):
        out_ref[piece, :, STATS:] = all_stats[piece * 4 : piece * 4 + 4]


def merge_four_call(pieces):
    return pl.pallas_call(
        merge_four_kernel,
        out_shape=jax.ShapeDtypeStruct((16, 4, ROW), BF16),
        in_specs=[VMEM_SPEC] * 4,
        out_specs=VMEM_SPEC,
        compiler_params=params(),
        cost_estimate=cost(2**20, 2 * 2**20),
        name="merge_four",
    )(*pieces)


def merge_yz_kernel(value_ref, out_ref):
    for clip in range(CLIPS):
        value, _, total = merge(
            clip,
            16,
            lambda k: value_ref[k, :, clip * HALF : clip * HALF + HALF].astype(F32),
            lambda k: value_ref[k, :, STATS:].astype(F32),
        )
        out_ref[clip] = (value / total).astype(BF16)


def merge_yz_call(arrived):
    return pl.pallas_call(
        merge_yz_kernel,
        out_shape=jax.ShapeDtypeStruct((CLIPS, 4, HALF), BF16),
        in_specs=[VMEM_SPEC],
        out_specs=VMEM_SPEC,
        compiler_params=params(),
        cost_estimate=cost(2**20, 2**19),
        name="merge_yz",
    )(arrived)


def flatten_kernel(value_ref, out_ref):
    for piece in range(16):
        out_ref[piece * 4 : piece * 4 + 4, :] = value_ref[piece]


def flatten_call(value):
    return pl.pallas_call(
        flatten_kernel,
        out_shape=jax.ShapeDtypeStruct((64, CLIPS * HALF), BF16),
        in_specs=[VMEM_SPEC],
        out_specs=VMEM_SPEC,
        compiler_params=params(),
        cost_estimate=cost(2**18, 2**20),
        name="flatten",
    )(value)


def mixed_half(clip, comb_ref, pieces):
    slots = jnp.concatenate([piece[:, column_slice(clip)] for piece in pieces], axis=0)
    return jnp.dot(comb_ref[clip], slots, preferred_element_type=F32).astype(BF16)


def mix_own_kernel(comb_ref, p0, p1, p2, p3, out_ref):
    for clip in range(CLIPS):
        out_ref[clip] = mixed_half(clip, comb_ref, (p0, p1, p2, p3))


def mix_own_call(comb, pieces):
    return pl.pallas_call(
        mix_own_kernel,
        out_shape=jax.ShapeDtypeStruct((CLIPS, TOK, HALF), BF16),
        in_specs=[VMEM_SPEC] * 5,
        out_specs=VMEM_SPEC,
        compiler_params=params(),
        cost_estimate=cost(2 * 1024 * 256 * 640, 4 * 2**20),
        name="mix_own",
    )(comb, *pieces)


def mix_all_kernel(where_ref, own_ref, comb_ref, p0, p1, p2, p3, out_hbm, half_ref, own_sem, sem):
    core = where_ref[0]
    copies = [
        pltpu.make_async_copy(own_ref.at[c], out_hbm.at[c, :, dynamic_half(core)], own_sem.at[c]) for c in range(CLIPS)
    ]
    for copy in copies:
        copy.start()
    for clip in range(CLIPS):
        half_ref[clip] = mixed_half(clip, comb_ref, (p0, p1, p2, p3))
        target = out_hbm.at[clip, :, dynamic_half(1 - core)]
        copies.append(pltpu.make_async_copy(half_ref.at[clip], target, sem.at[clip]))
        copies[-1].start()
    for copy in copies:
        copy.wait()


def mix_all_call(where, own, comb, pieces):
    return pl.pallas_call(
        mix_all_kernel,
        out_shape=jax.ShapeDtypeStruct((CLIPS, TOK, D), BF16),
        in_specs=[SMEM_SPEC] + [VMEM_SPEC] * 6,
        out_specs=HBM_SPEC,
        scratch_shapes=[
            pltpu.VMEM((CLIPS, TOK, HALF), BF16),
            pltpu.SemaphoreType.DMA((CLIPS,)),
            pltpu.SemaphoreType.DMA((CLIPS,)),
        ],
        compiler_params=params(),
        cost_estimate=cost(2 * 1024 * 256 * 640, 6 * 2**20),
        name="mix_all",
    )(where, own, comb, *pieces)


def targets(core, y, x, z):
    group = y * 2 + z % 2
    sent = [jnp.where(core == 0, (x + (0, 1, 3, 2)[k]) % 4, group ^ k) for k in range(4)]
    got = [jnp.where(core == 0, (x + (0, 3, 1, 2)[k]) % 4, group ^ k) for k in range(4)]
    return sent, got


def per_device(clips_x, slot_phi, w_in, b_in, w_out, b_out):
    me = lax.axis_index("seq")
    y, x, z, core = (c.astype(jnp.int32) for c in coords(me))
    mine = core * HALF
    to, got = targets(core, y, x, z)
    other_to, other_got = targets(1 - core, y, x, z)
    where = jnp.stack([core] + to + other_to + got + other_got)
    *sent, logits, dispatch, x_half = dispatch_call(where, clips_x, slot_phi)
    arrived = [swap_cores(piece) for piece in sent]
    own, stats = own_call(where, x_half, dispatch, sent)
    pieces = [send_piece(merge_cores_call(k, own, stats, arrived[k]), k) for k in SEND_ORDER[:3]]
    packed = merge_four_call([merge_cores_call(0, own, stats, arrived[0])] + pieces)
    packed = exchange(packed, STAGE_TWO)
    slot_in = merge_yz_call(packed).reshape(CLIPS * 4, HALF)
    partner = swap_cores(slot_in)
    rows = jnp.where(
        core == 0,
        jnp.concatenate([slot_in, partner], axis=1),
        jnp.concatenate([partner, slot_in], axis=1),
    )
    pre = jnp.dot(rows, w_in, preferred_element_type=F32)
    hidden = jax.nn.gelu(pre + b_in.astype(F32), approximate=False).astype(BF16)
    partial = jnp.dot(hidden, w_out, preferred_element_type=F32)
    part_mine = jnp.where(core == 0, partial[:, :HALF], partial[:, HALF:])
    part_theirs = jnp.where(core == 0, partial[:, HALF:], partial[:, :HALF])
    bias = lax.dynamic_slice(b_out, (me // 2, mine), (1, HALF)).astype(F32)
    summed = part_mine + swap_cores(part_theirs.astype(BF16)).astype(F32)
    slot_out = (summed + bias).astype(BF16)
    slot_out = slot_out.reshape(CLIPS, 4, HALF).transpose(1, 0, 2).reshape(1, 4, CLIPS * HALF)
    gathered = flatten_call(exchange(jnp.broadcast_to(slot_out, (16, 4, CLIPS * HALF)), STAGE_TWO))
    arriving = [send_piece(gathered, k) for k in SEND_ORDER[:3]]
    comb, other_comb, gathered = comb_call(where, logits, gathered)
    pieces = [gathered] + [arriving[SEND_ORDER.index(k)] for k in (1, 2, 3)]
    others = [swap_cores(piece) for piece in pieces]
    return mix_all_call(where, mix_own_call(comb, pieces), other_comb, others)


def solution(mesh):
    placed = (P("clip", "seq", None), P(), P(None, "seq"), P("seq"), P("seq", None), P())
    return jax.shard_map(
        per_device, mesh=mesh, in_specs=placed, out_specs=P("clip", "seq", None), check_vma=False
    )
```

```python
import functools

import jax
import jax.numpy as jnp
import numpy as np
from jax import lax
from jax.experimental import pallas as pl
from jax.experimental.pallas import tpu as pltpu
from jax.sharding import PartitionSpec as P

BF16 = jnp.bfloat16
F32 = jnp.float32
CLIPS = 4
SLOTS = 256
TOK = 256
D = 1280
EXPERTS = 64
HALF = 640
STATS = CLIPS * HALF
ROW = STATS + 128
VMEM_LIMIT = 8 * 2**20
LOAD_VMEM = 49 * 2**20
DISPATCH_VMEM = 16 * 2**20


def coords(index):
    return index // 64, index // 16 % 4, index // 2 % 8, index % 2


def groups_by(key):
    found = {}
    for index in range(128):
        found.setdefault(key(*coords(index)), []).append(index)
    return list(found.values())


STAGE_TWO = groups_by(lambda y, x, z, core: (core, x) if core == 0 else (core, y, z % 2))


def peer(index, k):
    y, x, z, core = coords(index)
    if core == 0:
        x = (x + (0, 1, 3, 2)[k]) % 4
    else:
        y, z = y ^ (k // 2), z ^ (k % 2)
    return ((y * 4 + x) * 8 + z) * 2 + core


def exchange(value, groups):
    return lax.all_to_all(value, "seq", 0, 0, tiled=True, axis_index_groups=groups)


def swap_cores(value):
    return lax.ppermute(value, "seq", [(source, source ^ 1) for source in range(128)])


def send_piece(value, k):
    return lax.ppermute(value, "seq", [(source, peer(source, k)) for source in range(128)])


def params(limit=VMEM_LIMIT):
    return pltpu.CompilerParams(vmem_limit_bytes=limit)


def cost(flops, bytes_accessed):
    return pl.CostEstimate(flops=flops, bytes_accessed=bytes_accessed, transcendentals=0)


def stats_lanes(clip, peak, total):
    p1 = peak.astype(BF16).astype(F32)
    p2 = (peak - p1).astype(BF16).astype(F32)
    p3 = peak - p1 - p2
    t1 = total.astype(BF16).astype(F32)
    t2 = total - t1
    lane = lax.broadcasted_iota(jnp.int32, (peak.shape[0], 128), 1) - 8 * clip
    out = jnp.where(lane == 0, p1, 0.0)
    for k, column in enumerate((p2, p3, t1, t2)):
        out = jnp.where(lane == k + 1, column, out)
    return out


def read_stats(clip, stats):
    lane = lax.broadcasted_iota(jnp.int32, stats.shape, stats.ndim - 1) - 8 * clip
    peak = jnp.sum(jnp.where((lane >= 0) & (lane < 3), stats, 0.0), axis=-1, keepdims=True)
    total = jnp.sum(jnp.where((lane >= 3) & (lane < 5), stats, 0.0), axis=-1, keepdims=True)
    return peak, total


def column_slice(clip):
    return slice(clip * HALF, clip * HALF + HALF)


def dynamic_half(core):
    return pl.ds(pl.multiple_of(core * HALF, 128), HALF)


def phi_rows(core):
    return pl.ds(pl.multiple_of(core * HALF, 128), HALF)


def order_matrix(core, where_ref, start):
    row = lax.broadcasted_iota(jnp.int32, (SLOTS, 1), 0)
    k, rest = row >> 6, row & 63
    piece = jnp.where(
        k < 2,
        jnp.where(k == 0, where_ref[start], where_ref[start + 1]),
        jnp.where(k == 2, where_ref[start + 2], where_ref[start + 3]),
    )
    by_x = ((rest >> 5) << 7) | (piece << 5) | (rest & 31)
    by_yz = ((piece >> 1) << 7) | ((rest >> 4) << 5) | (((rest >> 2) & 3) << 3) | ((piece & 1) << 2) | (rest & 3)
    slot = jnp.where(core == 0, by_x, by_yz)
    return jnp.where(lax.broadcasted_iota(jnp.int32, (SLOTS, SLOTS), 1) == slot, 1.0, 0.0).astype(BF16)


VMEM_SPEC = pl.BlockSpec(memory_space=pltpu.VMEM)
SMEM_SPEC = pl.BlockSpec(memory_space=pltpu.SMEM)
HBM_SPEC = pl.BlockSpec(memory_space=pltpu.HBM)
SENT, OTHER_SENT, GOT, OTHER_GOT, EXPERT = 1, 5, 9, 13, 17
SEND_ORDER = (3, 1, 2, 0)


def load_kernel(x_hbm, x_ref, sem):
    rows = TOK // 2
    copies = []
    for k in range(2 * CLIPS):
        at = (k // 2, pl.ds(k % 2 * rows, rows))
        copies.append(pltpu.make_async_copy(x_hbm.at[at], x_ref.at[at], sem.at[k]))
        copies[k].start()
    for copy in copies:
        copy.wait()


def load_call(clips_x):
    return pl.pallas_call(
        load_kernel,
        out_shape=jax.ShapeDtypeStruct((CLIPS, TOK, D), BF16),
        in_specs=[HBM_SPEC],
        out_specs=VMEM_SPEC,
        scratch_shapes=[pltpu.SemaphoreType.DMA((2 * CLIPS,))],
        compiler_params=params(LOAD_VMEM),
        cost_estimate=cost(0, 6 * 2**20),
        name="load",
    )(clips_x)


def dispatch_kernel(where_ref, x_ref, phi_ref, *refs):
    send_refs, (logits_ref, dispatch_ref) = refs[:4], refs[4:]
    core = where_ref[0]
    order = order_matrix(1 - core, where_ref, OTHER_SENT)
    tokens = x_ref[...].reshape(CLIPS * TOK, D)
    all_logits = jnp.dot(tokens, phi_ref[...], preferred_element_type=F32)
    stats = jnp.zeros((SLOTS, 128), F32)
    rounded = []
    for clip in range(CLIPS):
        logits = all_logits[clip * TOK : clip * TOK + TOK]
        logits_ref[clip] = logits
        peak = jnp.max(logits, axis=0, keepdims=True)
        expo = jnp.exp(logits - peak)
        total = jnp.sum(expo, axis=0, keepdims=True)
        rounded.append(expo.astype(BF16))
        both = jnp.concatenate([peak, total, jnp.zeros((6, SLOTS), F32)], axis=0).T
        stats += stats_lanes(clip, both[:, 0:1], both[:, 1:2])
    dispatch = lax.dot_general(
        order, jnp.concatenate(rounded, axis=0), (((1,), (1,)), ((), ())), preferred_element_type=F32
    ).astype(BF16)
    dispatch_ref[...] = dispatch
    for clip in range(CLIPS):
        part = dispatch[:, clip * TOK : clip * TOK + TOK]
        sums = jnp.dot(part, x_ref[clip, :, dynamic_half(1 - core)], preferred_element_type=F32).astype(BF16)
        for k in range(4):
            send_refs[k][:, column_slice(clip)] = sums[k * 64 : k * 64 + 64]
    stats = jnp.dot(order, stats.astype(BF16), preferred_element_type=F32).astype(BF16)
    for k in range(4):
        send_refs[k][:, STATS:] = stats[k * 64 : k * 64 + 64]


def dispatch_call(where, x, slot_phi):
    return pl.pallas_call(
        dispatch_kernel,
        out_shape=tuple(jax.ShapeDtypeStruct((64, ROW), BF16) for _ in range(4))
        + (
            jax.ShapeDtypeStruct((CLIPS, TOK, SLOTS), F32),
            jax.ShapeDtypeStruct((SLOTS, CLIPS * TOK), BF16),
        ),
        in_specs=[SMEM_SPEC] + [VMEM_SPEC] * 2,
        out_specs=(VMEM_SPEC,) * 6,
        compiler_params=params(DISPATCH_VMEM),
        cost_estimate=cost(2 * 1024 * 256 * 1920, 6 * 2**20),
        name="dispatch",
    )(where, x, slot_phi)


def own_kernel(where_ref, x_ref, dispatch_ref, s0, s1, s2, s3, own_ref, stats_ref):
    core = where_ref[0]
    given = order_matrix(1 - core, where_ref, OTHER_SENT)
    order = order_matrix(core, where_ref, SENT)
    order = lax.dot_general(order, given, (((1,), (1,)), ((), ())), preferred_element_type=F32).astype(BF16)
    stats = jnp.concatenate([s[:, STATS:] for s in (s0, s1, s2, s3)], axis=0)
    stats_ref[...] = jnp.dot(order, stats, preferred_element_type=F32).astype(BF16)
    dispatch = jnp.dot(order, dispatch_ref[...], preferred_element_type=F32).astype(BF16)
    for clip in range(CLIPS):
        part = dispatch[:, clip * TOK : clip * TOK + TOK]
        own_ref[:, column_slice(clip)] = jnp.dot(part, x_ref[clip, :, dynamic_half(core)], preferred_element_type=F32)


def own_call(where, x, dispatch, sent):
    return pl.pallas_call(
        own_kernel,
        out_shape=(
            jax.ShapeDtypeStruct((SLOTS, CLIPS * HALF), F32),
            jax.ShapeDtypeStruct((SLOTS, 128), BF16),
        ),
        in_specs=[SMEM_SPEC] + [VMEM_SPEC] * 6,
        out_specs=(VMEM_SPEC,) * 2,
        compiler_params=params(),
        cost_estimate=cost(2 * 1024 * 256 * 640, 6 * 2**20),
        name="own_half",
    )(where, x, dispatch, *sent)


def comb_kernel(where_ref, logits_ref, piece_ref, comb_ref, other_comb_ref, same_ref):
    core = where_ref[0]
    same_ref[...] = piece_ref[...]
    orders = order_matrix(core, where_ref, GOT), order_matrix(1 - core, where_ref, OTHER_GOT)
    for clip in range(CLIPS):
        logits = logits_ref[clip]
        weights = jnp.exp(logits - jnp.max(logits, axis=1, keepdims=True))
        comb = (weights / jnp.sum(weights, axis=1, keepdims=True)).astype(BF16)
        for order, out_ref in zip(orders, (comb_ref, other_comb_ref)):
            turned = lax.dot_general(comb, order, (((1,), (1,)), ((), ())), preferred_element_type=F32)
            out_ref[clip] = turned.astype(BF16)


def comb_call(where, logits, piece):
    return pl.pallas_call(
        comb_kernel,
        out_shape=(
            jax.ShapeDtypeStruct((CLIPS, TOK, SLOTS), BF16),
            jax.ShapeDtypeStruct((CLIPS, TOK, SLOTS), BF16),
            jax.ShapeDtypeStruct((64, CLIPS * HALF), BF16),
        ),
        in_specs=[SMEM_SPEC] + [VMEM_SPEC] * 2,
        out_specs=(VMEM_SPEC,) * 3,
        compiler_params=params(),
        cost_estimate=cost(2**27, 4 * 2**20),
        name="comb",
    )(where, logits, piece)


def expert_in_kernel(where_ref, slot_in_ref, partner_ref, w_ref, b_ref, hidden_ref):
    core = where_ref[0]
    pre = jnp.dot(slot_in_ref[...], w_ref[phi_rows(core), :], preferred_element_type=F32)
    pre += jnp.dot(partner_ref[...], w_ref[phi_rows(1 - core), :], preferred_element_type=F32)
    pre += b_ref[...].astype(F32)
    hidden_ref[...] = (0.5 * pre * (1.0 + lax.erf(pre * np.float32(np.sqrt(0.5))))).astype(BF16)


def expert_in_call(where, slot_in, partner, w_in, b_in):
    return pl.pallas_call(
        expert_in_kernel,
        out_shape=jax.ShapeDtypeStruct((CLIPS * 4, D), BF16),
        in_specs=[SMEM_SPEC] + [VMEM_SPEC] * 4,
        out_specs=VMEM_SPEC,
        compiler_params=params(),
        cost_estimate=cost(2 * 16 * D * D, 4 * 2**20),
        name="expert_in",
    )(where, slot_in, partner, w_in, b_in)


def expert_out_kernel(where_ref, hidden_ref, w_ref, b_ref, mine_ref, theirs_ref):
    core = where_ref[0]
    hidden = hidden_ref[...]
    expert = lax.broadcasted_iota(jnp.int32, (CLIPS * 4, EXPERTS), 1) == where_ref[EXPERT]
    bias = jnp.dot(
        jnp.where(expert, 1.0, 0.0).astype(BF16), b_ref[:, dynamic_half(core)], preferred_element_type=F32
    )
    theirs_ref[...] = jnp.dot(hidden, w_ref[:, dynamic_half(1 - core)], preferred_element_type=F32).astype(BF16)
    mine_ref[...] = jnp.dot(hidden, w_ref[:, dynamic_half(core)], preferred_element_type=F32) + bias


def expert_out_call(where, hidden, w_out, b_out):
    return pl.pallas_call(
        expert_out_kernel,
        out_shape=(
            jax.ShapeDtypeStruct((CLIPS * 4, HALF), F32),
            jax.ShapeDtypeStruct((CLIPS * 4, HALF), BF16),
        ),
        in_specs=[SMEM_SPEC] + [VMEM_SPEC] * 3,
        out_specs=(VMEM_SPEC,) * 2,
        compiler_params=params(),
        cost_estimate=cost(2 * 16 * D * D, 4 * 2**20),
        name="expert_out",
    )(where, hidden, w_out, b_out)


def merge_cores_kernel(k, own_ref, mine_ref, arrived_ref, out_ref):
    rows = slice(k * 64, k * 64 + 64)
    mine = mine_ref[rows].astype(F32)
    theirs = arrived_ref[:, STATS:].astype(F32)
    stats = jnp.zeros(mine.shape, F32)
    for clip in range(CLIPS):
        peak_a, total_a = read_stats(clip, mine)
        peak_b, total_b = read_stats(clip, theirs)
        peak = jnp.maximum(peak_a, peak_b)
        fa = jnp.exp(peak_a - peak)
        fb = jnp.exp(peak_b - peak)
        at = column_slice(clip)
        out_ref[:, at] = (fa * own_ref[rows, at] + fb * arrived_ref[:, at].astype(F32)).astype(BF16)
        stats += stats_lanes(clip, peak, fa * total_a + fb * total_b)
    out_ref[:, STATS:] = stats.astype(BF16)


def merge_cores_call(k, own, mine, arrived):
    return pl.pallas_call(
        functools.partial(merge_cores_kernel, k),
        out_shape=jax.ShapeDtypeStruct((64, ROW), BF16),
        in_specs=[VMEM_SPEC] * 3,
        out_specs=VMEM_SPEC,
        compiler_params=params(),
        cost_estimate=cost(2**20, 2**20),
        name="merge_cores",
    )(own, mine, arrived)


def merge(clip, sources, value_of, stats_of):
    stats = [read_stats(clip, stats_of(k)) for k in range(sources)]
    peak = stats[0][0]
    for p, _ in stats[1:]:
        peak = jnp.maximum(peak, p)
    value, total = None, None
    for k, (p, t) in enumerate(stats):
        factor = jnp.exp(p - peak)
        v = factor * value_of(k)
        value = v if k == 0 else value + v
        total = factor * t if k == 0 else total + factor * t
    return value, peak, total


def merge_four_kernel(*refs):
    piece_refs, out_ref = refs[:4], refs[4]
    all_stats = jnp.zeros((64, 128), F32)
    for clip in range(CLIPS):
        at = column_slice(clip)
        value, peak, total = merge(
            clip,
            4,
            lambda k: piece_refs[k][:, at].astype(F32),
            lambda k: piece_refs[k][:, STATS:].astype(F32),
        )
        value = value.astype(BF16)
        all_stats += stats_lanes(clip, peak, total)
        for piece in range(16):
            out_ref[piece, :, at] = value[piece * 4 : piece * 4 + 4]
    all_stats = all_stats.astype(BF16)
    for piece in range(16):
        out_ref[piece, :, STATS:] = all_stats[piece * 4 : piece * 4 + 4]


def merge_four_call(pieces):
    return pl.pallas_call(
        merge_four_kernel,
        out_shape=jax.ShapeDtypeStruct((16, 4, ROW), BF16),
        in_specs=[VMEM_SPEC] * 4,
        out_specs=VMEM_SPEC,
        compiler_params=params(),
        cost_estimate=cost(2**20, 2 * 2**20),
        name="merge_four",
    )(*pieces)


def merge_yz_kernel(value_ref, out_ref):
    for clip in range(CLIPS):
        value, _, total = merge(
            clip,
            16,
            lambda k: value_ref[k, :, clip * HALF : clip * HALF + HALF].astype(F32),
            lambda k: value_ref[k, :, STATS:].astype(F32),
        )
        out_ref[clip] = (value / total).astype(BF16)


def merge_yz_call(arrived):
    return pl.pallas_call(
        merge_yz_kernel,
        out_shape=jax.ShapeDtypeStruct((CLIPS, 4, HALF), BF16),
        in_specs=[VMEM_SPEC],
        out_specs=VMEM_SPEC,
        compiler_params=params(),
        cost_estimate=cost(2**20, 2**19),
        name="merge_yz",
    )(arrived)


def flatten_kernel(value_ref, out_ref):
    for piece in range(16):
        out_ref[piece * 4 : piece * 4 + 4, :] = value_ref[piece]


def flatten_call(value):
    return pl.pallas_call(
        flatten_kernel,
        out_shape=jax.ShapeDtypeStruct((64, CLIPS * HALF), BF16),
        in_specs=[VMEM_SPEC],
        out_specs=VMEM_SPEC,
        compiler_params=params(),
        cost_estimate=cost(2**18, 2**20),
        name="flatten",
    )(value)


def mixed_half(clip, comb_ref, pieces):
    slots = jnp.concatenate([piece[:, column_slice(clip)] for piece in pieces], axis=0)
    return jnp.dot(comb_ref[clip], slots, preferred_element_type=F32).astype(BF16)


def mix_own_kernel(comb_ref, p0, p1, p2, p3, out_ref):
    for clip in range(CLIPS):
        out_ref[clip] = mixed_half(clip, comb_ref, (p0, p1, p2, p3))


def mix_own_call(comb, pieces):
    return pl.pallas_call(
        mix_own_kernel,
        out_shape=jax.ShapeDtypeStruct((CLIPS, TOK, HALF), BF16),
        in_specs=[VMEM_SPEC] * 5,
        out_specs=VMEM_SPEC,
        compiler_params=params(),
        cost_estimate=cost(2 * 1024 * 256 * 640, 4 * 2**20),
        name="mix_own",
    )(comb, *pieces)


def mix_all_kernel(where_ref, own_ref, comb_ref, p0, p1, p2, p3, out_hbm, half_ref, own_sem, sem):
    core = where_ref[0]
    copies = [
        pltpu.make_async_copy(own_ref.at[c], out_hbm.at[c, :, dynamic_half(core)], own_sem.at[c]) for c in range(CLIPS)
    ]
    for copy in copies:
        copy.start()
    for clip in range(CLIPS):
        half_ref[clip] = mixed_half(clip, comb_ref, (p0, p1, p2, p3))
        target = out_hbm.at[clip, :, dynamic_half(1 - core)]
        copies.append(pltpu.make_async_copy(half_ref.at[clip], target, sem.at[clip]))
        copies[-1].start()
    for copy in copies:
        copy.wait()


def mix_all_call(where, own, comb, pieces):
    return pl.pallas_call(
        mix_all_kernel,
        out_shape=jax.ShapeDtypeStruct((CLIPS, TOK, D), BF16),
        in_specs=[SMEM_SPEC] + [VMEM_SPEC] * 6,
        out_specs=HBM_SPEC,
        scratch_shapes=[
            pltpu.VMEM((CLIPS, TOK, HALF), BF16),
            pltpu.SemaphoreType.DMA((CLIPS,)),
            pltpu.SemaphoreType.DMA((CLIPS,)),
        ],
        compiler_params=params(),
        cost_estimate=cost(2 * 1024 * 256 * 640, 6 * 2**20),
        name="mix_all",
    )(where, own, comb, *pieces)


def targets(core, y, x, z):
    group = y * 2 + z % 2
    sent = [jnp.where(core == 0, (x + (0, 1, 3, 2)[k]) % 4, group ^ k) for k in range(4)]
    got = [jnp.where(core == 0, (x + (0, 3, 1, 2)[k]) % 4, group ^ k) for k in range(4)]
    return sent, got


def per_device(clips_x, slot_phi, w_in, b_in, w_out, b_out):
    me = lax.axis_index("seq")
    y, x, z, core = (c.astype(jnp.int32) for c in coords(me))
    to, got = targets(core, y, x, z)
    other_to, other_got = targets(1 - core, y, x, z)
    where = jnp.stack([core] + to + other_to + got + other_got + [(me // 2).astype(jnp.int32)])
    tokens = load_call(clips_x)
    *sent, logits, dispatch = dispatch_call(where, tokens, slot_phi)
    arrived = [swap_cores(piece) for piece in sent]
    own, stats = own_call(where, tokens, dispatch, sent)
    pieces = [send_piece(merge_cores_call(k, own, stats, arrived[k]), k) for k in SEND_ORDER[:3]]
    packed = merge_four_call([merge_cores_call(0, own, stats, arrived[0])] + pieces)
    packed = exchange(packed, STAGE_TWO)
    slot_in = merge_yz_call(packed).reshape(CLIPS * 4, HALF)
    partner = swap_cores(slot_in)
    hidden = expert_in_call(where, slot_in, partner, w_in, b_in[None])
    part_mine, part_theirs = expert_out_call(where, hidden, w_out, b_out)
    slot_out = (part_mine + swap_cores(part_theirs).astype(F32)).astype(BF16)
    slot_out = slot_out.reshape(CLIPS, 4, HALF).transpose(1, 0, 2).reshape(1, 4, CLIPS * HALF)
    gathered = flatten_call(exchange(jnp.broadcast_to(slot_out, (16, 4, CLIPS * HALF)), STAGE_TWO))
    arriving = [send_piece(gathered, k) for k in SEND_ORDER[:3]]
    comb, other_comb, gathered = comb_call(where, logits, gathered)
    pieces = [gathered] + [arriving[SEND_ORDER.index(k)] for k in (1, 2, 3)]
    others = [swap_cores(piece) for piece in pieces]
    return mix_all_call(where, mix_own_call(comb, pieces), other_comb, others)


def solution(mesh):
    placed = (P("clip", "seq", None), P(), P(None, "seq"), P("seq"), P("seq", None), P())
    return jax.shard_map(
        per_device, mesh=mesh, in_specs=placed, out_specs=P("clip", "seq", None), check_vma=False
    )
```

```python
import functools

import jax
import jax.numpy as jnp
import numpy as np
from jax import lax
from jax.experimental import pallas as pl
from jax.experimental.pallas import tpu as pltpu
from jax.sharding import PartitionSpec as P

BF16 = jnp.bfloat16
F32 = jnp.float32
CLIPS = 4
SLOTS = 256
TOK = 256
D = 1280
EXPERTS = 64
HALF = 640
STATS = CLIPS * HALF
ROW = STATS + 128
VMEM_LIMIT = 8 * 2**20
LOAD_VMEM = 49 * 2**20
DISPATCH_VMEM = 16 * 2**20


def coords(index):
    return index // 64, index // 16 % 4, index // 2 % 8, index % 2


def groups_by(key):
    found = {}
    for index in range(128):
        found.setdefault(key(*coords(index)), []).append(index)
    return list(found.values())


def second_rank(index):
    y, x, z, core = coords(index)
    return z * 2 + y if core == 0 else z // 2 * 4 + x


STAGE_TWO = [
    sorted(group, key=second_rank)
    for group in groups_by(lambda y, x, z, core: (core, x) if core == 0 else (core, y, z % 2))
]


def peer(index, k):
    y, x, z, core = coords(index)
    if core == 0:
        x = (x + (0, 1, 3, 2)[k]) % 4
    else:
        y, z = y ^ (k // 2), z ^ (k % 2)
    return ((y * 4 + x) * 8 + z) * 2 + core


def exchange(value, groups):
    return lax.all_to_all(value, "seq", 0, 0, tiled=True, axis_index_groups=groups)


def swap_cores(value):
    return lax.ppermute(value, "seq", [(source, source ^ 1) for source in range(128)])


def send_piece(value, k):
    return lax.ppermute(value, "seq", [(source, peer(source, k)) for source in range(128)])


def params(limit=VMEM_LIMIT):
    return pltpu.CompilerParams(vmem_limit_bytes=limit)


def cost(flops, bytes_accessed):
    return pl.CostEstimate(flops=flops, bytes_accessed=bytes_accessed, transcendentals=0)


def stats_lanes(clip, peak, total):
    p1 = peak.astype(BF16).astype(F32)
    p2 = (peak - p1).astype(BF16).astype(F32)
    p3 = peak - p1 - p2
    t1 = total.astype(BF16).astype(F32)
    t2 = total - t1
    lane = lax.broadcasted_iota(jnp.int32, (peak.shape[0], 128), 1) - 8 * clip
    out = jnp.where(lane == 0, p1, 0.0)
    for k, column in enumerate((p2, p3, t1, t2)):
        out = jnp.where(lane == k + 1, column, out)
    return out


def read_stats(clip, stats):
    lane = lax.broadcasted_iota(jnp.int32, stats.shape, stats.ndim - 1) - 8 * clip
    peak = jnp.sum(jnp.where((lane >= 0) & (lane < 3), stats, 0.0), axis=-1, keepdims=True)
    total = jnp.sum(jnp.where((lane >= 3) & (lane < 5), stats, 0.0), axis=-1, keepdims=True)
    return peak, total


def column_slice(clip):
    return slice(clip * HALF, clip * HALF + HALF)


def dynamic_half(core):
    return pl.ds(pl.multiple_of(core * HALF, 128), HALF)


def phi_rows(core):
    return pl.ds(pl.multiple_of(core * HALF, 128), HALF)


def order_matrix(core, where_ref, start):
    row = lax.broadcasted_iota(jnp.int32, (SLOTS, 1), 0)
    k, rest = row >> 6, row & 63
    piece = jnp.where(
        k < 2,
        jnp.where(k == 0, where_ref[start], where_ref[start + 1]),
        jnp.where(k == 2, where_ref[start + 2], where_ref[start + 3]),
    )
    by_x = (((rest >> 2) & 1) << 7) | (piece << 5) | ((rest >> 3) << 2) | (rest & 3)
    by_yz = ((piece >> 1) << 7) | (((rest >> 2) & 3) << 5) | ((rest >> 4) << 3) | ((piece & 1) << 2) | (rest & 3)
    slot = jnp.where(core == 0, by_x, by_yz)
    return jnp.where(lax.broadcasted_iota(jnp.int32, (SLOTS, SLOTS), 1) == slot, 1.0, 0.0).astype(BF16)


VMEM_SPEC = pl.BlockSpec(memory_space=pltpu.VMEM)
SMEM_SPEC = pl.BlockSpec(memory_space=pltpu.SMEM)
HBM_SPEC = pl.BlockSpec(memory_space=pltpu.HBM)
SENT, OTHER_SENT, GOT, OTHER_GOT, EXPERT = 1, 5, 9, 13, 17
SEND_ORDER = (3, 1, 2, 0)


def load_kernel(x_hbm, x_ref, sem):
    rows = TOK // 2
    copies = []
    for k in range(2 * CLIPS):
        at = (k // 2, pl.ds(k % 2 * rows, rows))
        copies.append(pltpu.make_async_copy(x_hbm.at[at], x_ref.at[at], sem.at[k]))
        copies[k].start()
    for copy in copies:
        copy.wait()


def load_call(clips_x):
    return pl.pallas_call(
        load_kernel,
        out_shape=jax.ShapeDtypeStruct((CLIPS, TOK, D), BF16),
        in_specs=[HBM_SPEC],
        out_specs=VMEM_SPEC,
        scratch_shapes=[pltpu.SemaphoreType.DMA((2 * CLIPS,))],
        compiler_params=params(LOAD_VMEM),
        cost_estimate=cost(0, 6 * 2**20),
        name="load",
    )(clips_x)


def dispatch_kernel(where_ref, x_ref, phi_ref, *refs):
    send_refs, (logits_ref, dispatch_ref, order_ref) = refs[:4], refs[4:]
    core = where_ref[0]
    order = order_matrix(1 - core, where_ref, OTHER_SENT)
    order_ref[...] = lax.dot_general(
        order_matrix(core, where_ref, SENT), order, (((1,), (1,)), ((), ())), preferred_element_type=F32
    ).astype(BF16)
    tokens = x_ref[...].reshape(CLIPS * TOK, D)
    all_logits = jnp.dot(tokens, phi_ref[...], preferred_element_type=F32)
    stats = jnp.zeros((SLOTS, 128), F32)
    rounded = []
    for clip in range(CLIPS):
        logits = all_logits[clip * TOK : clip * TOK + TOK]
        logits_ref[clip] = logits
        peak = jnp.max(logits, axis=0, keepdims=True)
        expo = jnp.exp(logits - peak)
        total = jnp.sum(expo, axis=0, keepdims=True)
        rounded.append(expo.astype(BF16))
        both = jnp.concatenate([peak, total, jnp.zeros((6, SLOTS), F32)], axis=0).T
        stats += stats_lanes(clip, both[:, 0:1], both[:, 1:2])
    dispatch = lax.dot_general(
        order, jnp.concatenate(rounded, axis=0), (((1,), (1,)), ((), ())), preferred_element_type=F32
    ).astype(BF16)
    dispatch_ref[...] = dispatch
    for clip in range(CLIPS):
        part = dispatch[:, clip * TOK : clip * TOK + TOK]
        sums = jnp.dot(part, x_ref[clip, :, dynamic_half(1 - core)], preferred_element_type=F32).astype(BF16)
        for k in range(4):
            send_refs[k][:, column_slice(clip)] = sums[k * 64 : k * 64 + 64]
    stats = jnp.dot(order, stats.astype(BF16), preferred_element_type=F32).astype(BF16)
    for k in range(4):
        send_refs[k][:, STATS:] = stats[k * 64 : k * 64 + 64]


def dispatch_call(where, x, slot_phi):
    return pl.pallas_call(
        dispatch_kernel,
        out_shape=tuple(jax.ShapeDtypeStruct((64, ROW), BF16) for _ in range(4))
        + (
            jax.ShapeDtypeStruct((CLIPS, TOK, SLOTS), F32),
            jax.ShapeDtypeStruct((SLOTS, CLIPS * TOK), BF16),
            jax.ShapeDtypeStruct((SLOTS, SLOTS), BF16),
        ),
        in_specs=[SMEM_SPEC] + [VMEM_SPEC] * 2,
        out_specs=(VMEM_SPEC,) * 7,
        compiler_params=params(DISPATCH_VMEM),
        cost_estimate=cost(2 * 1024 * 256 * 1920, 6 * 2**20),
        name="dispatch",
    )(where, x, slot_phi)


def own_kernel(where_ref, x_ref, dispatch_ref, order_ref, s0, s1, s2, s3, own_ref, stats_ref):
    core = where_ref[0]
    order = order_ref[...]
    stats = jnp.concatenate([s[:, STATS:] for s in (s0, s1, s2, s3)], axis=0)
    stats_ref[...] = jnp.dot(order, stats, preferred_element_type=F32).astype(BF16)
    dispatch = jnp.dot(order, dispatch_ref[...], preferred_element_type=F32).astype(BF16)
    for clip in range(CLIPS):
        part = dispatch[:, clip * TOK : clip * TOK + TOK]
        own_ref[:, column_slice(clip)] = jnp.dot(part, x_ref[clip, :, dynamic_half(core)], preferred_element_type=F32)


def own_call(where, x, dispatch, order, sent):
    return pl.pallas_call(
        own_kernel,
        out_shape=(
            jax.ShapeDtypeStruct((SLOTS, CLIPS * HALF), F32),
            jax.ShapeDtypeStruct((SLOTS, 128), BF16),
        ),
        in_specs=[SMEM_SPEC] + [VMEM_SPEC] * 7,
        out_specs=(VMEM_SPEC,) * 2,
        compiler_params=params(),
        cost_estimate=cost(2 * 1024 * 256 * 640, 6 * 2**20),
        name="own_half",
    )(where, x, dispatch, order, *sent)


def comb_kernel(where_ref, logits_ref, piece_ref, comb_ref, other_comb_ref, same_ref):
    core = where_ref[0]
    same_ref[...] = piece_ref[...]
    orders = order_matrix(core, where_ref, GOT), order_matrix(1 - core, where_ref, OTHER_GOT)
    for clip in range(CLIPS):
        logits = logits_ref[clip]
        weights = jnp.exp(logits - jnp.max(logits, axis=1, keepdims=True))
        comb = (weights / jnp.sum(weights, axis=1, keepdims=True)).astype(BF16)
        for order, out_ref in zip(orders, (comb_ref, other_comb_ref)):
            turned = lax.dot_general(comb, order, (((1,), (1,)), ((), ())), preferred_element_type=F32)
            out_ref[clip] = turned.astype(BF16)


def comb_call(where, logits, piece):
    return pl.pallas_call(
        comb_kernel,
        out_shape=(
            jax.ShapeDtypeStruct((CLIPS, TOK, SLOTS), BF16),
            jax.ShapeDtypeStruct((CLIPS, TOK, SLOTS), BF16),
            jax.ShapeDtypeStruct((64, CLIPS * HALF), BF16),
        ),
        in_specs=[SMEM_SPEC] + [VMEM_SPEC] * 2,
        out_specs=(VMEM_SPEC,) * 3,
        compiler_params=params(),
        cost_estimate=cost(2**27, 4 * 2**20),
        name="comb",
    )(where, logits, piece)


def expert_in_kernel(where_ref, slot_in_ref, partner_ref, w_ref, b_ref, hidden_ref):
    core = where_ref[0]
    pre = jnp.dot(slot_in_ref[...], w_ref[phi_rows(core), :], preferred_element_type=F32)
    pre += jnp.dot(partner_ref[...], w_ref[phi_rows(1 - core), :], preferred_element_type=F32)
    pre += b_ref[...].astype(F32)
    hidden_ref[...] = (0.5 * pre * (1.0 + lax.erf(pre * np.float32(np.sqrt(0.5))))).astype(BF16)


def expert_in_call(where, slot_in, partner, w_in, b_in):
    return pl.pallas_call(
        expert_in_kernel,
        out_shape=jax.ShapeDtypeStruct((CLIPS * 4, D), BF16),
        in_specs=[SMEM_SPEC] + [VMEM_SPEC] * 4,
        out_specs=VMEM_SPEC,
        compiler_params=params(),
        cost_estimate=cost(2 * 16 * D * D, 4 * 2**20),
        name="expert_in",
    )(where, slot_in, partner, w_in, b_in)


def expert_out_kernel(where_ref, hidden_ref, w_ref, b_ref, mine_ref, theirs_ref):
    core = where_ref[0]
    hidden = hidden_ref[...]
    expert = lax.broadcasted_iota(jnp.int32, (CLIPS * 4, EXPERTS), 1) == where_ref[EXPERT]
    bias = jnp.dot(
        jnp.where(expert, 1.0, 0.0).astype(BF16), b_ref[:, dynamic_half(core)], preferred_element_type=F32
    )
    theirs_ref[...] = jnp.dot(hidden, w_ref[:, dynamic_half(1 - core)], preferred_element_type=F32).astype(BF16)
    mine_ref[...] = jnp.dot(hidden, w_ref[:, dynamic_half(core)], preferred_element_type=F32) + bias


def expert_out_call(where, hidden, w_out, b_out):
    return pl.pallas_call(
        expert_out_kernel,
        out_shape=(
            jax.ShapeDtypeStruct((CLIPS * 4, HALF), F32),
            jax.ShapeDtypeStruct((CLIPS * 4, HALF), BF16),
        ),
        in_specs=[SMEM_SPEC] + [VMEM_SPEC] * 3,
        out_specs=(VMEM_SPEC,) * 2,
        compiler_params=params(),
        cost_estimate=cost(2 * 16 * D * D, 4 * 2**20),
        name="expert_out",
    )(where, hidden, w_out, b_out)


def merge_cores_kernel(k, own_ref, mine_ref, arrived_ref, out_ref):
    rows = slice(k * 64, k * 64 + 64)
    mine = mine_ref[rows].astype(F32)
    theirs = arrived_ref[:, STATS:].astype(F32)
    stats = jnp.zeros(mine.shape, F32)
    for clip in range(CLIPS):
        peak_a, total_a = read_stats(clip, mine)
        peak_b, total_b = read_stats(clip, theirs)
        peak = jnp.maximum(peak_a, peak_b)
        fa = jnp.exp(peak_a - peak)
        fb = jnp.exp(peak_b - peak)
        at = column_slice(clip)
        out_ref[:, at] = (fa * own_ref[rows, at] + fb * arrived_ref[:, at].astype(F32)).astype(BF16)
        stats += stats_lanes(clip, peak, fa * total_a + fb * total_b)
    out_ref[:, STATS:] = stats.astype(BF16)


def merge_cores_call(k, own, mine, arrived):
    return pl.pallas_call(
        functools.partial(merge_cores_kernel, k),
        out_shape=jax.ShapeDtypeStruct((64, ROW), BF16),
        in_specs=[VMEM_SPEC] * 3,
        out_specs=VMEM_SPEC,
        compiler_params=params(),
        cost_estimate=cost(2**20, 2**20),
        name="merge_cores",
    )(own, mine, arrived)


def merge(clip, sources, value_of, stats_of):
    stats = [read_stats(clip, stats_of(k)) for k in range(sources)]
    peak = stats[0][0]
    for p, _ in stats[1:]:
        peak = jnp.maximum(peak, p)
    value, total = None, None
    for k, (p, t) in enumerate(stats):
        factor = jnp.exp(p - peak)
        v = factor * value_of(k)
        value = v if k == 0 else value + v
        total = factor * t if k == 0 else total + factor * t
    return value, peak, total


def merge_four_kernel(*refs):
    piece_refs, out_ref = refs[:4], refs[4]
    all_stats = jnp.zeros((64, 128), F32)
    for clip in range(CLIPS):
        at = column_slice(clip)
        value, peak, total = merge(
            clip,
            4,
            lambda k: piece_refs[k][:, at].astype(F32),
            lambda k: piece_refs[k][:, STATS:].astype(F32),
        )
        value = value.astype(BF16)
        all_stats += stats_lanes(clip, peak, total)
        for piece in range(16):
            out_ref[piece, :, at] = value[piece * 4 : piece * 4 + 4]
    all_stats = all_stats.astype(BF16)
    for piece in range(16):
        out_ref[piece, :, STATS:] = all_stats[piece * 4 : piece * 4 + 4]


def merge_four_call(pieces):
    return pl.pallas_call(
        merge_four_kernel,
        out_shape=jax.ShapeDtypeStruct((16, 4, ROW), BF16),
        in_specs=[VMEM_SPEC] * 4,
        out_specs=VMEM_SPEC,
        compiler_params=params(),
        cost_estimate=cost(2**20, 2 * 2**20),
        name="merge_four",
    )(*pieces)


def merge_yz_kernel(value_ref, out_ref):
    for clip in range(CLIPS):
        value, _, total = merge(
            clip,
            16,
            lambda k: value_ref[k, :, clip * HALF : clip * HALF + HALF].astype(F32),
            lambda k: value_ref[k, :, STATS:].astype(F32),
        )
        out_ref[clip] = (value / total).astype(BF16)


def merge_yz_call(arrived):
    return pl.pallas_call(
        merge_yz_kernel,
        out_shape=jax.ShapeDtypeStruct((CLIPS, 4, HALF), BF16),
        in_specs=[VMEM_SPEC],
        out_specs=VMEM_SPEC,
        compiler_params=params(),
        cost_estimate=cost(2**20, 2**19),
        name="merge_yz",
    )(arrived)


def flatten_kernel(value_ref, out_ref):
    for piece in range(16):
        out_ref[piece * 4 : piece * 4 + 4, :] = value_ref[piece]


def flatten_call(value):
    return pl.pallas_call(
        flatten_kernel,
        out_shape=jax.ShapeDtypeStruct((64, CLIPS * HALF), BF16),
        in_specs=[VMEM_SPEC],
        out_specs=VMEM_SPEC,
        compiler_params=params(),
        cost_estimate=cost(2**18, 2**20),
        name="flatten",
    )(value)


def mixed_half(clip, comb_ref, pieces):
    slots = jnp.concatenate([piece[:, column_slice(clip)] for piece in pieces], axis=0)
    return jnp.dot(comb_ref[clip], slots, preferred_element_type=F32).astype(BF16)


def mix_own_kernel(comb_ref, p0, p1, p2, p3, out_ref):
    for clip in range(CLIPS):
        out_ref[clip] = mixed_half(clip, comb_ref, (p0, p1, p2, p3))


def mix_own_call(comb, pieces):
    return pl.pallas_call(
        mix_own_kernel,
        out_shape=jax.ShapeDtypeStruct((CLIPS, TOK, HALF), BF16),
        in_specs=[VMEM_SPEC] * 5,
        out_specs=VMEM_SPEC,
        compiler_params=params(),
        cost_estimate=cost(2 * 1024 * 256 * 640, 4 * 2**20),
        name="mix_own",
    )(comb, *pieces)


def mix_all_kernel(where_ref, own_ref, comb_ref, p0, p1, p2, p3, out_hbm, half_ref, own_sem, sem):
    core = where_ref[0]
    copies = [
        pltpu.make_async_copy(own_ref.at[c], out_hbm.at[c, :, dynamic_half(core)], own_sem.at[c]) for c in range(CLIPS)
    ]
    for copy in copies:
        copy.start()
    for clip in range(CLIPS):
        half_ref[clip] = mixed_half(clip, comb_ref, (p0, p1, p2, p3))
        target = out_hbm.at[clip, :, dynamic_half(1 - core)]
        copies.append(pltpu.make_async_copy(half_ref.at[clip], target, sem.at[clip]))
        copies[-1].start()
    for copy in copies:
        copy.wait()


def mix_all_call(where, own, comb, pieces):
    return pl.pallas_call(
        mix_all_kernel,
        out_shape=jax.ShapeDtypeStruct((CLIPS, TOK, D), BF16),
        in_specs=[SMEM_SPEC] + [VMEM_SPEC] * 6,
        out_specs=HBM_SPEC,
        scratch_shapes=[
            pltpu.VMEM((CLIPS, TOK, HALF), BF16),
            pltpu.SemaphoreType.DMA((CLIPS,)),
            pltpu.SemaphoreType.DMA((CLIPS,)),
        ],
        compiler_params=params(),
        cost_estimate=cost(2 * 1024 * 256 * 640, 6 * 2**20),
        name="mix_all",
    )(where, own, comb, *pieces)


def targets(core, y, x, z):
    group = y * 2 + z % 2
    sent = [jnp.where(core == 0, (x + (0, 1, 3, 2)[k]) % 4, group ^ k) for k in range(4)]
    got = [jnp.where(core == 0, (x + (0, 3, 1, 2)[k]) % 4, group ^ k) for k in range(4)]
    return sent, got


def per_device(clips_x, slot_phi, w_in, b_in, w_out, b_out):
    me = lax.axis_index("seq")
    y, x, z, core = (c.astype(jnp.int32) for c in coords(me))
    to, got = targets(core, y, x, z)
    other_to, other_got = targets(1 - core, y, x, z)
    where = jnp.stack([core] + to + other_to + got + other_got + [(me // 2).astype(jnp.int32)])
    tokens = load_call(clips_x)
    *sent, logits, dispatch, order = dispatch_call(where, tokens, slot_phi)
    arrived = [swap_cores(piece) for piece in sent]
    own, stats = own_call(where, tokens, dispatch, order, sent)
    pieces = [send_piece(merge_cores_call(k, own, stats, arrived[k]), k) for k in SEND_ORDER[:3]]
    packed = merge_four_call([merge_cores_call(0, own, stats, arrived[0])] + pieces)
    packed = exchange(packed, STAGE_TWO)
    slot_in = merge_yz_call(packed).reshape(CLIPS * 4, HALF)
    partner = swap_cores(slot_in)
    hidden = expert_in_call(where, slot_in, partner, w_in, b_in[None])
    part_mine, part_theirs = expert_out_call(where, hidden, w_out, b_out)
    slot_out = (part_mine + swap_cores(part_theirs).astype(F32)).astype(BF16)
    slot_out = slot_out.reshape(CLIPS, 4, HALF).transpose(1, 0, 2).reshape(1, 4, CLIPS * HALF)
    gathered = flatten_call(exchange(jnp.broadcast_to(slot_out, (16, 4, CLIPS * HALF)), STAGE_TWO))
    arriving = [send_piece(gathered, k) for k in SEND_ORDER[:3]]
    comb, other_comb, gathered = comb_call(where, logits, gathered)
    pieces = [gathered] + [arriving[SEND_ORDER.index(k)] for k in (1, 2, 3)]
    others = [swap_cores(piece) for piece in pieces]
    return mix_all_call(where, mix_own_call(comb, pieces), other_comb, others)


def solution(mesh):
    placed = (P("clip", "seq", None), P(), P(None, "seq"), P("seq"), P("seq", None), P())
    return jax.shard_map(
        per_device, mesh=mesh, in_specs=placed, out_specs=P("clip", "seq", None), check_vma=False
    )
```
